32 devices in a mesh: aux: 4 (over y, core), row: 8 (over z, x).
Axes of the slice: x: 2, y: 2, z: 4, core: 2. Of those that a mesh axis runs over, the one named last changes fastest.
Arguments:
- integrals: bfloat16 [16, 16, 4, 256, 256], P('aux', 'row'), may hold values from -6 to 6
- block_columns: int32 [16, 4], P('row'), may hold values from 0 to 15, as said below
- orbitals: bfloat16 [4096, 2048], P('row'), may hold values from -0.1875 to 0.1875
- occ_mask: int32 [16, 8], replicated, may hold values from 0 to 1, as said below
Outputs:
- exchange: float32 [4096, 1536], P('row', 'aux')
The draws below stay inside these ranges and needn't reach their ends.
Inputs may be any that keep to these rules, and one draw needn't show every extreme that they name: `block_columns`: each row block has 4 different column blocks, each lying on the same row device as the row block or on the one beside it. `occ_mask`: entry (b, s) is 1 when row block b lies on row device s, and 0 when it lies on a device more than one away from s.
All inputs are finite; a program needn't handle non-finite values.
Results may differ from the reference program's by a relative error of at most 0.0018.
Values may be sent and summed in bfloat16 or wider, within the bound.
A program may use at most 128 MiB of HBM per device.

```python
import jax
import jax.numpy as jnp
from jax import lax

MU_DEV = 512
BS = 256
KEPT = 4
NOCC = 2048
NAUX = 16
NBF = 4096
RB = 2
NB = 16
OB = 256
N_ROW = 8


def draw_block_columns(key, part):
    scores = jax.random.randint(key, (NB, 3 * RB), 0, 1 << 20)
    scores = scores * (3 * RB) + jnp.arange(3 * RB, dtype=jnp.int32)[None, :]
    device = jnp.arange(NB, dtype=jnp.int32) // RB
    column = (device[:, None] - 1) * RB + jnp.arange(3 * RB, dtype=jnp.int32)[None, :]
    usable = (column >= 0) & (column < NB)
    scores = jnp.where(usable, scores, scores + (1 << 28))
    ranked = jnp.argsort(scores, axis=1, stable=True)[:, :KEPT]
    return jnp.take_along_axis(column, ranked, axis=1).astype(jnp.int32)


def draw_occ_mask(key, part):
    tosses = jax.random.randint(key, (NB, N_ROW), 0, 4)
    owners = jnp.arange(NB, dtype=jnp.int32)[:, None] // RB
    slices = jnp.arange(N_ROW, dtype=jnp.int32)[None, :]
    distance = jnp.abs(owners - slices)
    nearby = jnp.where(tosses > 0, 1, 0)
    return jnp.where(distance == 0, 1, jnp.where(distance == 1, nearby, 0)).astype(jnp.int32)


def level_of(own_key, extent, pieces, low, top_value):
    loudness = 1.0
    for position, blocks in pieces:
        draws = jax.random.uniform(jax.random.fold_in(jax.random.fold_in(own_key, 6), position), (blocks,), jnp.float32, low / len(pieces), top_value / len(pieces))
        loudness = loudness * jnp.repeat(jnp.exp(draws), extent[position] // blocks).reshape((-1,) + (1,) * (len(extent) - 1 - position))
    return loudness


def scatter_about(rng, shape, deviation, reach, split=(), kind=jnp.bfloat16):
    level = level_of(rng, shape, split, -0.22, 0.18) if split else 1.0
    array = jax.random.normal(rng, shape, jnp.float32) * deviation * level
    return jnp.minimum(jnp.maximum(array, -reach), reach).astype(kind)


def setup_inputs(seed: int = 0) -> dict:
    streams_of = jax.random.split(jax.random.key(seed), 5)
    return {
        "integrals": scatter_about(streams_of[0], (NAUX, NB, KEPT, BS, BS), 1.0, 6.0, ((0, 4), (1, 8))),
        "block_columns": draw_block_columns(jax.random.fold_in(streams_of[4], 71), 0),
        "orbitals": scatter_about(streams_of[2], (NBF, NOCC), (KEPT * BS) ** -0.5, 0.1875, ((0, 8),)),
        "occ_mask": draw_occ_mask(jax.random.fold_in(streams_of[4], 71), 0),
    }


def reference(integrals, block_columns, orbitals, occ_mask):
    weight_scale = 1.0 / (NAUX * OB) ** 0.5
    orbital_blocks = orbitals.reshape(NB, BS, NOCC)

    def window_half(source):
        occupied = lax.dynamic_slice_in_dim(orbital_blocks, source * OB, OB, 2)
        stacked = []
        for place in range(3):
            neighbor = source - 1 + place
            inside = ((neighbor >= 0) & (neighbor < N_ROW)).astype(jnp.float32)
            clipped = jnp.clip(neighbor, 0, N_ROW - 1).astype(jnp.int32)
            blocks = lax.dynamic_slice_in_dim(integrals, clipped * RB, RB, 1)
            columns = lax.dynamic_slice_in_dim(block_columns, clipped * RB, RB, 0)
            picked = occupied[columns]
            half = jnp.einsum('prkml,rklj->pjrm', blocks.astype(jnp.float32), picked.astype(jnp.float32))
            mask_rows = lax.dynamic_slice_in_dim(occ_mask, clipped * RB, RB, 0)
            factor = lax.dynamic_slice_in_dim(mask_rows, source, 1, 1)[:, 0].astype(jnp.float32) * inside
            half = half * factor[None, None, :, None]
            stacked.append(half.reshape(NAUX, OB, MU_DEV))
        return jnp.concatenate(stacked, 2).astype(jnp.bfloat16)

    windows = lax.map(window_half, jnp.arange(N_ROW, dtype=jnp.int32))

    def owner_rows(owner):
        summed = jnp.zeros((MU_DEV, 3 * MU_DEV), jnp.float32)
        for place in range(3):
            source = owner + 1 - place
            inside = ((source >= 0) & (source < N_ROW)).astype(jnp.float32)
            clipped = jnp.clip(source, 0, N_ROW - 1).astype(jnp.int32)
            window = lax.dynamic_index_in_dim(windows, clipped, 0, keepdims=False).astype(jnp.float32)
            strip_rows = window[:, :, place * MU_DEV:(place + 1) * MU_DEV]
            strip = jnp.einsum('pjm,pjn->mn', strip_rows, window) * weight_scale
            framed = jnp.pad(strip, ((0, 0), (MU_DEV, MU_DEV)))[:, place * MU_DEV:place * MU_DEV + 3 * MU_DEV]
            summed = summed + inside * framed
        return summed

    result = lax.map(owner_rows, jnp.arange(N_ROW, dtype=jnp.int32))
    return result.reshape(NBF, 3 * MU_DEV)
```

```python
import functools

import jax
import jax.numpy as jnp
from jax import lax
from jax.experimental import pallas as pl
from jax.experimental.pallas import tpu as pltpu
from jax.sharding import PartitionSpec as P

MESH = pl.DeviceIdType.MESH
NT = (((1,), (1,)), ((), ()))


def overlap(lo, hi, start, stop):
    lo, hi = max(lo, start), min(hi, stop)
    return (lo, hi) if lo < hi else None


def kernel(
    aux,
    rows,
    scale,
    cols_ref,
    mask_ref,
    orb_ref,
    int_hbm,
    out_ref,
    ints,
    e0,
    e1,
    e2,
    h0,
    h1,
    h2,
    rh0,
    rh1,
    d_buf,
    w_buf,
    v_buf,
    s_rec,
    v_rec,
    int_sem,
    orb_send,
    orb_recv,
    fwd_send,
    fwd_recv,
    h_send,
    h_recv,
    d_send,
    d_recv,
    w_send,
    w_recv,
    v_send,
    v_recv,
):
    a = lax.axis_index("aux")
    r = lax.axis_index("row")
    naux, nb, kept, bs, _ = ints.shape
    own = nb * bs
    half = aux // 2
    quota = out_ref.shape[0]
    core = lax.rem(a, 2)
    sibling = a + 1 - 2 * core
    low = a < half
    g = jnp.where(low, 0, 2)
    has_left = r > 0
    has_right = r < rows - 1
    source_row = jnp.where(low, r - 1, r + 1)
    target_row = jnp.where(low, r + 1, r - 1)
    has_source = jnp.where(low, r, rows - 1 - r) > 0
    has_target = jnp.where(low, rows - 1 - r, r) > 0
    slots = (1, 2 - g, g)
    ext = (e0, e1, e2)
    held = (h0, h1, h2)
    came = (rh0, rh1)

    load = pltpu.make_async_copy(int_hbm, ints, int_sem)
    load.start()

    barrier = pltpu.get_barrier_semaphore()

    def greet(device):
        pl.semaphore_signal(barrier, inc=1, device_id=device, device_id_type=MESH)

    @pl.when(has_left)
    def _():
        greet((a, r - 1))

    @pl.when(has_right)
    def _():
        greet((a, r + 1))

    for step in range(1, aux):
        greet((lax.rem(a + step, aux), r))

    @pl.when(has_source)
    def _():
        for place in range(half):
            greet((jnp.where(low, half + place, place), source_row))

    greeted = jnp.where(has_left, 1, 0) + jnp.where(has_right, 1, 0)
    greeted += jnp.where(has_source, half, 0) + aux - 1
    pl.semaphore_wait(barrier, greeted)

    def remote(src, dst, send, recv, device):
        return pltpu.make_async_remote_copy(
            src_ref=src,
            dst_ref=dst,
            send_sem=send,
            recv_sem=recv,
            device_id=device,
            device_id_type=MESH,
        )

    def orb_right(i):
        return remote(
            orb_ref.at[slots[i] + 2, core],
            ext[i].at[core],
            orb_send.at[i, 0],
            orb_recv.at[i, 0],
            (a, r + 1),
        )

    def orb_left(i):
        return remote(
            orb_ref.at[slots[i], core],
            ext[i].at[2 * nb + core],
            orb_send.at[i, 1],
            orb_recv.at[i, 1],
            (a, r - 1),
        )

    def forward(i, side):
        block = ext[i].at[2 * nb * side + core]
        return remote(block, block, fwd_send.at[i, side], fwd_recv.at[i, side], (sibling, r))

    def forwarded(i, side):
        block = ext[i].at[2 * nb * side + 1 - core]
        return remote(block, block, fwd_send.at[i, side], fwd_recv.at[i, side], (sibling, r))

    def send_orbitals(i):
        @pl.when(has_right)
        def _():
            orb_right(i).start()

        @pl.when(has_left)
        def _():
            orb_left(i).start()

    def share_orbitals(i):
        ext[i][nb : 2 * nb] = orb_ref[slots[i] + 1]

        @pl.when(has_left)
        def _():
            orb_right(i).wait_recv()
            forward(i, 0).start()

        @pl.when(has_right)
        def _():
            orb_left(i).wait_recv()
            forward(i, 1).start()

    def await_orbitals(i):
        @pl.when(has_left)
        def _():
            forwarded(i, 0).wait_recv()

        @pl.when(has_right)
        def _():
            forwarded(i, 1).wait_recv()

    def transform(i, b):
        factor = mask_ref[b, slots[i]]
        columns = [cols_ref[b, k] for k in range(kept)]

        @pl.loop(0, naux)
        def _(p):
            total = jnp.zeros((bs, held[i].shape[-1]), jnp.float32)
            for k in range(kept):
                total += jnp.dot(
                    ints[p, b, k], ext[i][columns[k]], preferred_element_type=jnp.float32
                )
            held[i][b, p] = (total * factor).astype(jnp.bfloat16)

    def half_copy(i, b):
        return remote(
            held[i].at[b], came[i].at[b], h_send.at[i, b], h_recv.at[i, b], (a, target_row)
        )

    def send_half(i, b):
        @pl.when(has_target)
        def _():
            half_copy(i, b).start()

    def product(pairs):
        def add(p, total):
            for left, lb, right, rb in pairs:
                total += lax.dot_general(
                    left[lb, p], right[rb, p], NT, preferred_element_type=jnp.float32
                )
            return total

        return lax.fori_loop(0, naux, add, jnp.zeros((bs, bs), jnp.float32)) * scale

    def part_of(owner, base, start, stop):
        return overlap(base + start, base + stop, owner * quota, (owner + 1) * quota)

    def diagonal_copy(owner, contributor, span):
        lo, hi = span
        return remote(
            d_buf.at[pl.ds(lo - own, hi - lo)],
            s_rec.at[contributor, pl.ds(lo - owner * quota, hi - lo)],
            d_send.at[owner],
            d_recv.at[contributor],
            (owner, r),
        )

    def beside_copy(owner, contributor, span, base, b):
        lo, hi = span
        return remote(
            w_buf.at[b, pl.ds(lo - base - b * bs, hi - lo)],
            s_rec.at[contributor, pl.ds(lo - owner * quota, hi - lo)],
            w_send.at[owner, b],
            w_recv.at[contributor, b],
            (owner, r),
        )

    def turned_copy(owner, place, span, base, b):
        lo, hi = span
        return remote(
            v_buf.at[b, pl.ds(lo - base, hi - lo)],
            v_rec.at[place, b, pl.ds(lo - owner * quota, hi - lo)],
            v_send.at[owner, b],
            v_recv.at[place, b],
            (owner, source_row),
        )

    def each_diagonal(act):
        for owner in range(aux):
            span = part_of(owner, own, 0, own)
            if span is not None:

                @pl.when(a != owner)
                def _():
                    act(diagonal_copy(owner, a, span))

    def each_beside(b, act):
        for in_low, base in ((True, 0), (False, 2 * own)):

            @pl.when(jnp.logical_and(has_source, low if in_low else jnp.logical_not(low)))
            def _():
                for owner in range(aux):
                    span = part_of(owner, base, b * bs, (b + 1) * bs)
                    if span is not None:

                        @pl.when(a != owner)
                        def _():
                            act(beside_copy(owner, a, span, base, b))

    def each_turned(b, act):
        for in_low, base in ((True, 2 * own), (False, 0)):

            @pl.when(jnp.logical_and(has_source, low if in_low else jnp.logical_not(low)))
            def _():
                for owner in range(aux):
                    span = part_of(owner, base, 0, own)
                    if span is not None:
                        act(turned_copy(owner, lax.rem(a, half), span, base, b))

    def start(copy):
        copy.start()

    def wait_send(copy):
        copy.wait_send()

    send_orbitals(0)
    send_orbitals(1)
    share_orbitals(0)
    load.wait()
    await_orbitals(0)
    transform(0, 0)
    send_half(0, 0)
    share_orbitals(1)
    transform(0, 1)
    await_orbitals(1)
    transform(1, 0)
    send_half(1, 0)
    send_orbitals(2)
    transform(1, 1)
    for i in range(2):
        send_half(i, 1)
    share_orbitals(2)
    await_orbitals(2)
    for b in range(nb):
        transform(2, b)

    for b in range(nb):
        for other in range(nb):
            d_buf[b * bs : (b + 1) * bs, other * bs : (other + 1) * bs] = product(
                [(h, b, h, other) for h in held]
            )
    each_diagonal(start)

    for b in range(nb):

        @pl.when(has_source)
        def _():
            half_copy(0, b).wait_recv()
            half_copy(1, b).wait_recv()
            for other in range(nb):
                v_buf[b, other * bs : (other + 1) * bs] = product(
                    [(h2, other, rh0, b), (h0, other, rh1, b)]
                ).astype(jnp.bfloat16)

        each_turned(b, start)

        @pl.when(has_source)
        def _():
            for other in range(nb):
                w_buf[b, :, other * bs : (other + 1) * bs] = product(
                    [(rh0, b, h2, other), (rh1, b, h0, other)]
                )

        each_beside(b, start)

    for owner in range(aux):

        @pl.when(a == owner)
        def _():
            first = owner * quota
            span = part_of(owner, own, 0, own)
            if span is not None:
                lo, hi = span
                total = d_buf[lo - own : hi - own]
                for peer in range(aux):
                    if peer != owner:
                        diagonal_copy(owner, peer, span).wait_recv()
                        total += s_rec[peer, lo - first : hi - first]
                out_ref[lo - first : hi - first] = total
            base = 0 if owner < half else 2 * own
            group = range(half) if owner < half else range(half, aux)
            whole = part_of(owner, base, 0, own)
            if whole is not None:

                @pl.when(jnp.logical_not(has_source))
                def _():
                    lo, hi = whole
                    out_ref[lo - first : hi - first] = jnp.zeros(
                        (hi - lo, out_ref.shape[1]), jnp.float32
                    )

                @pl.when(has_source)
                def _():
                    for b in range(nb):
                        span = part_of(owner, base, b * bs, (b + 1) * bs)
                        if span is not None:
                            lo, hi = span
                            shift = base + b * bs
                            total = w_buf[b, lo - shift : hi - shift]
                            for peer in group:
                                if peer != owner:
                                    beside_copy(owner, peer, span, base, b).wait_recv()
                                    total += s_rec[peer, lo - first : hi - first]
                            out_ref[lo - first : hi - first] = total
                    lo, hi = whole
                    for b in range(nb):
                        for place in range(half):
                            turned_copy(owner, place, whole, base, b).wait_recv()
                            out_ref[lo - first : hi - first, b * bs : (b + 1) * bs] += v_rec[
                                place, b, lo - first : hi - first
                            ].astype(jnp.float32)

    for i in range(3):

        @pl.when(has_right)
        def _():
            orb_right(i).wait_send()
            forward(i, 1).wait_send()

        @pl.when(has_left)
        def _():
            orb_left(i).wait_send()
            forward(i, 0).wait_send()

    @pl.when(has_target)
    def _():
        for i in range(2):
            for b in range(nb):
                half_copy(i, b).wait_send()

    each_diagonal(wait_send)
    for b in range(nb):
        each_turned(b, wait_send)
        each_beside(b, wait_send)


def on_device(integrals, block_columns, orbitals, occ_mask):
    naux, nb, kept, bs, _ = integrals.shape
    own, occ_count = orbitals.shape
    aux = lax.axis_size("aux")
    rows = lax.axis_size("row")
    r = lax.axis_index("row")
    width = occ_count // rows
    scale = 1.0 / (naux * aux * width) ** 0.5
    quota = 3 * own // aux
    near = [
        lax.dynamic_slice_in_dim(orbitals, jnp.clip(r + step, 0, rows - 1) * width, width, 1)
        for step in range(-2, 3)
    ]
    orb = jnp.stack(near, 0).reshape(5, nb, bs, width)
    cols = block_columns - (r - 1) * nb
    slices = r - 1 + jnp.arange(3)
    inside = (slices >= 0) & (slices < rows)
    mask_rows = lax.dynamic_slice_in_dim(occ_mask, r * nb, nb, 0).astype(jnp.float32)
    mask = mask_rows[:, jnp.clip(slices, 0, rows - 1)] * inside.astype(jnp.float32)[None]
    ext = pltpu.VMEM((3 * nb, bs, width), jnp.bfloat16)
    held = pltpu.VMEM((nb, naux, bs, width), jnp.bfloat16)
    dma = pltpu.SemaphoreType.DMA
    flops = 2 * naux * bs * bs * width * nb * (3 * kept + 7 * nb)
    turned = pl.pallas_call(
        functools.partial(kernel, aux, rows, scale),
        out_shape=jax.ShapeDtypeStruct((quota, own), jnp.float32),
        in_specs=[
            pl.BlockSpec(memory_space=pltpu.SMEM),
            pl.BlockSpec(memory_space=pltpu.SMEM),
            pl.BlockSpec(memory_space=pltpu.VMEM),
            pl.BlockSpec(memory_space=pl.ANY),
        ],
        out_specs=pl.BlockSpec(memory_space=pltpu.VMEM),
        scratch_shapes=[pltpu.VMEM(integrals.shape, jnp.bfloat16)]
        + [ext] * 3
        + [held] * 5
        + [
            pltpu.VMEM((own, own), jnp.float32),
            pltpu.VMEM((nb, bs, own), jnp.float32),
            pltpu.VMEM((nb, own, bs), jnp.bfloat16),
            pltpu.VMEM((aux, quota, own), jnp.float32),
            pltpu.VMEM((aux // 2, nb, quota, bs), jnp.bfloat16),
            dma,
            dma((3, 2)),
            dma((3, 2)),
            dma((3, 2)),
            dma((3, 2)),
            dma((2, nb)),
            dma((2, nb)),
            dma((aux,)),
            dma((aux,)),
            dma((aux, nb)),
            dma((aux, nb)),
            dma((aux, nb)),
            dma((aux // 2, nb)),
        ],
        compiler_params=pltpu.CompilerParams(
            collective_id=0, has_side_effects=True, vmem_limit_bytes=48 * 1024 * 1024
        ),
        cost_estimate=pl.CostEstimate(
            flops=flops, bytes_accessed=2 * integrals.size, transcendentals=0
        ),
    )(cols, mask, orb, integrals)
    return turned.T


def solution(mesh):
    in_specs = (P("aux", "row", None, None, None), P("row", None), P("row", None), P())
    out_specs = P("row", "aux")
    return jax.shard_map(
        on_device, mesh=mesh, in_specs=in_specs, out_specs=out_specs, check_vma=False
    )
```

```python
import functools

import jax
import jax.numpy as jnp
from jax import lax
from jax.experimental import pallas as pl
from jax.experimental.pallas import tpu as pltpu
from jax.sharding import PartitionSpec as P

MESH = pl.DeviceIdType.MESH
NT = (((1,), (1,)), ((), ()))


def overlap(lo, hi, start, stop):
    lo, hi = max(lo, start), min(hi, stop)
    return (lo, hi) if lo < hi else None


def kernel(
    aux,
    rows,
    scale,
    cols_ref,
    mask_ref,
    orb_hbm,
    int_hbm,
    out_ref,
    ints,
    orb_ref,
    e0,
    e1,
    e2,
    h0,
    h1,
    h2,
    rh0,
    rh1,
    d_buf,
    w_buf,
    v_buf,
    s_rec,
    v_rec,
    int_sem,
    near_sem,
    orb_send,
    orb_recv,
    fwd_send,
    fwd_recv,
    h_send,
    h_recv,
    d_send,
    d_recv,
    w_send,
    w_recv,
    v_send,
    v_recv,
):
    a = lax.axis_index("aux")
    r = lax.axis_index("row")
    naux, nb, kept, bs, _ = ints.shape
    own = nb * bs
    width = e0.shape[-1]
    share = own // aux
    per_block = bs // share
    piece = w_buf.shape[1]
    chunks = own // piece
    half = aux // 2
    quota = out_ref.shape[0]
    low = a < half
    has_left = r > 0
    has_right = r < rows - 1
    source_row = jnp.where(low, r - 1, r + 1)
    target_row = jnp.where(low, r + 1, r - 1)
    has_source = jnp.where(low, r, rows - 1 - r) > 0
    has_target = jnp.where(low, rows - 1 - r, r) > 0
    ext = (e0, e1, e2)
    held = (h0, h1, h2)
    came = (rh0, rh1)

    load = pltpu.make_async_copy(int_hbm, ints, int_sem)
    load.start()
    near = []
    for t in range(5):
        if len(orb_hbm.shape) == 2:
            column = jnp.clip(r - 2 + t, 0, rows - 1) * width
            source = orb_hbm.at[:, pl.ds(pl.multiple_of(column, width), width)]
        else:
            source = orb_hbm.at[t]
        near.append(pltpu.make_async_copy(source, orb_ref.at[t], near_sem.at[t]))
        near[t].start()

    barrier = pltpu.get_barrier_semaphore()

    def greet(device):
        pl.semaphore_signal(barrier, inc=1, device_id=device, device_id_type=MESH)

    @pl.when(has_left)
    def _():
        greet((a, r - 1))

    @pl.when(has_right)
    def _():
        greet((a, r + 1))

    for step in range(1, aux):
        greet((lax.rem(a + step, aux), r))

    @pl.when(has_source)
    def _():
        for place in range(half):
            greet((jnp.where(low, half + place, place), source_row))

    greeted = jnp.where(has_left, 1, 0) + jnp.where(has_right, 1, 0)
    greeted += jnp.where(has_source, half, 0) + aux - 1
    pl.semaphore_wait(barrier, greeted)

    def remote(src, dst, send, recv, device):
        return pltpu.make_async_remote_copy(
            src_ref=src,
            dst_ref=dst,
            send_sem=send,
            recv_sem=recv,
            device_id=device,
            device_id_type=MESH,
        )

    def quarter(i, side, contributor):
        first = pl.multiple_of(lax.rem(contributor, per_block) * share, share)
        return ext[i].at[2 * nb * side + contributor // per_block, pl.ds(first, share)]

    mine = pl.ds(pl.multiple_of(a * share, share), share)

    def orb_right(i):
        return remote(
            orb_ref.at[i + 2, mine],
            quarter(i, 0, a),
            orb_send.at[i, 0],
            orb_recv.at[i, 0],
            (a, r + 1),
        )

    def orb_left(i):
        return remote(
            orb_ref.at[i, mine],
            quarter(i, 1, a),
            orb_send.at[i, 1],
            orb_recv.at[i, 1],
            (a, r - 1),
        )

    def forward(i, side, step, contributor):
        block = quarter(i, side, contributor)
        return remote(
            block,
            block,
            fwd_send.at[i, side, step - 1],
            fwd_recv.at[i, side, step - 1],
            (lax.rem(a + step, aux), r),
        )

    def send_orbitals(i):
        @pl.when(has_right)
        def _():
            orb_right(i).start()

        @pl.when(has_left)
        def _():
            orb_left(i).start()

    def share_orbitals(i):
        @pl.when(has_left)
        def _():
            orb_right(i).wait_recv()
            for step in range(1, aux):
                forward(i, 0, step, a).start()

        @pl.when(has_right)
        def _():
            orb_left(i).wait_recv()
            for step in range(1, aux):
                forward(i, 1, step, a).start()

        for b in range(nb):
            ext[i][nb + b] = orb_ref[i + 1, b * bs : (b + 1) * bs]

    def await_orbitals(i):
        for side, there in ((0, has_left), (1, has_right)):

            @pl.when(there)
            def _():
                for step in range(1, aux):
                    forward(i, side, step, lax.rem(a + aux - step, aux)).wait_recv()

    def by_half(i, act):
        if i == 0:
            act(1)
        else:

            @pl.when(low)
            def _():
                act(4 - 2 * i)

            @pl.when(jnp.logical_not(low))
            def _():
                act(2 * i - 2)

    def transform(i, b):
        by_half(i, lambda slot: transform_slot(i, slot, b))

    def transform_slot(i, slot, b):
        at = r - 1 + slot
        inside = jnp.logical_and(at >= 0, at < rows)
        held_here = mask_ref[r * nb + b, jnp.clip(at, 0, rows - 1)]
        factor = jnp.where(inside, held_here, 0).astype(jnp.float32)
        columns = [jnp.clip(cols_ref[b, k] - (r - 1) * nb, 0, 3 * nb - 1) for k in range(kept)]

        @pl.loop(0, naux)
        def _(p):
            total = jnp.zeros((bs, held[i].shape[-1]), jnp.float32)
            for k in range(kept):
                total += jnp.dot(
                    ints[p, b, k], ext[slot][columns[k]], preferred_element_type=jnp.float32
                )
            held[i][b, p] = (total * factor).astype(jnp.bfloat16)

    def piece_of(c):
        start = c * piece % bs
        return c * piece // bs, slice(start, start + piece)

    def half_copy(i, c):
        b, inner = piece_of(c)
        inner = pl.ds(inner.start, piece)
        return remote(
            held[i].at[b, :, inner],
            came[i].at[b, :, inner],
            h_send.at[i, c],
            h_recv.at[i, c],
            (a, target_row),
        )

    def send_half(i, b):
        @pl.when(has_target)
        def _():
            for c in range(b * bs // piece, (b + 1) * bs // piece):
                half_copy(i, c).start()

    def product(pairs, shape):
        def add(p, total):
            for left, lb, li, right, rb, ri in pairs:
                total += lax.dot_general(
                    left[lb, p, li], right[rb, p, ri], NT, preferred_element_type=jnp.float32
                )
            return total

        return lax.fori_loop(0, naux, add, jnp.zeros(shape, jnp.float32)) * scale

    def part_of(owner, base, start, stop):
        return overlap(base + start, base + stop, owner * quota, (owner + 1) * quota)

    def diagonal_copy(owner, contributor, span):
        lo, hi = span
        return remote(
            d_buf.at[pl.ds(lo - own, hi - lo)],
            s_rec.at[contributor, pl.ds(lo - owner * quota, hi - lo)],
            d_send.at[owner],
            d_recv.at[contributor],
            (owner, r),
        )

    def beside_copy(owner, contributor, span, base, b):
        lo, hi = span
        return remote(
            w_buf.at[b, pl.ds(lo - base - b * piece, hi - lo)],
            s_rec.at[contributor, pl.ds(lo - owner * quota, hi - lo)],
            w_send.at[owner, b],
            w_recv.at[contributor, b],
            (owner, r),
        )

    def turned_copy(owner, place, span, base, b):
        lo, hi = span
        return remote(
            v_buf.at[b, pl.ds(lo - base, hi - lo)],
            v_rec.at[place, b, pl.ds(lo - owner * quota, hi - lo)],
            v_send.at[owner, b],
            v_recv.at[place, b],
            (owner, source_row),
        )

    def each_diagonal(act):
        for owner in range(aux):
            span = part_of(owner, own, 0, own)
            if span is not None:

                @pl.when(a != owner)
                def _():
                    act(diagonal_copy(owner, a, span))

    def each_beside(b, act):
        for in_low, base in ((True, 0), (False, 2 * own)):

            @pl.when(jnp.logical_and(has_source, low if in_low else jnp.logical_not(low)))
            def _():
                for owner in range(aux):
                    span = part_of(owner, base, b * piece, (b + 1) * piece)
                    if span is not None:

                        @pl.when(a != owner)
                        def _():
                            act(beside_copy(owner, a, span, base, b))

    def each_turned(b, act):
        for in_low, base in ((True, 2 * own), (False, 0)):

            @pl.when(jnp.logical_and(has_source, low if in_low else jnp.logical_not(low)))
            def _():
                for owner in range(aux):
                    span = part_of(owner, base, 0, own)
                    if span is not None:
                        act(turned_copy(owner, lax.rem(a, half), span, base, b))

    def start(copy):
        copy.start()

    def wait_send(copy):
        copy.wait_send()

    for copy in near:
        copy.wait()
    for slot in (1, 0, 2):
        send_orbitals(slot)
    for slot in (1, 0, 2):
        share_orbitals(slot)
    load.wait()
    by_half(0, await_orbitals)
    transform(0, 0)
    send_half(0, 0)
    by_half(1, await_orbitals)
    transform(1, 0)
    send_half(1, 0)
    for b in range(1, nb):
        for i in range(2):
            transform(i, b)
            send_half(i, b)
    by_half(2, await_orbitals)
    for b in range(nb):
        transform(2, b)

    full = slice(0, bs)
    for b in range(nb):
        for other in range(nb):
            d_buf[b * bs : (b + 1) * bs, other * bs : (other + 1) * bs] = product(
                [(h, b, full, h, other, full) for h in held], (bs, bs)
            )
    each_diagonal(start)

    for c in range(chunks):
        b, inner = piece_of(c)

        @pl.when(has_source)
        def _():
            half_copy(0, c).wait_recv()
            half_copy(1, c).wait_recv()
            for other in range(nb):
                v_buf[c, other * bs : (other + 1) * bs] = product(
                    [(h2, other, full, rh0, b, inner), (h0, other, full, rh1, b, inner)],
                    (bs, piece),
                ).astype(jnp.bfloat16)

        each_turned(c, start)

        @pl.when(has_source)
        def _():
            for other in range(nb):
                w_buf[c, :, other * bs : (other + 1) * bs] = product(
                    [(rh0, b, inner, h2, other, full), (rh1, b, inner, h0, other, full)],
                    (piece, bs),
                )

        each_beside(c, start)

    for owner in range(aux):

        @pl.when(a == owner)
        def _():
            first = owner * quota
            span = part_of(owner, own, 0, own)
            if span is not None:
                lo, hi = span
                total = d_buf[lo - own : hi - own]
                for peer in range(aux):
                    if peer != owner:
                        diagonal_copy(owner, peer, span).wait_recv()
                        total += s_rec[peer, lo - first : hi - first]
                out_ref[lo - first : hi - first] = total
            base = 0 if owner < half else 2 * own
            group = range(half) if owner < half else range(half, aux)
            whole = part_of(owner, base, 0, own)
            if whole is not None:

                @pl.when(jnp.logical_not(has_source))
                def _():
                    lo, hi = whole
                    out_ref[lo - first : hi - first] = jnp.zeros(
                        (hi - lo, out_ref.shape[1]), jnp.float32
                    )

                @pl.when(has_source)
                def _():
                    for b in range(chunks):
                        span = part_of(owner, base, b * piece, (b + 1) * piece)
                        if span is not None:
                            lo, hi = span
                            shift = base + b * piece
                            total = w_buf[b, lo - shift : hi - shift]
                            for peer in group:
                                if peer != owner:
                                    beside_copy(owner, peer, span, base, b).wait_recv()
                                    total += s_rec[peer, lo - first : hi - first]
                            out_ref[lo - first : hi - first] = total
                    lo, hi = whole
                    for b in range(chunks):
                        for place in range(half):
                            turned_copy(owner, place, whole, base, b).wait_recv()
                            out_ref[lo - first : hi - first, b * piece : (b + 1) * piece] += v_rec[
                                place, b, lo - first : hi - first
                            ].astype(jnp.float32)

    for i in range(3):
        for side, there, copy in ((0, has_left, orb_left), (1, has_right, orb_right)):

            @pl.when(there)
            def _():
                copy(i).wait_send()
                for step in range(1, aux):
                    forward(i, side, step, a).wait_send()

    @pl.when(has_target)
    def _():
        for i in range(2):
            for c in range(chunks):
                half_copy(i, c).wait_send()

    each_diagonal(wait_send)
    for c in range(chunks):
        each_turned(c, wait_send)
        each_beside(c, wait_send)


def on_device(integrals, block_columns, orbitals, occ_mask):
    naux, nb, kept, bs, _ = integrals.shape
    own, occ_count = orbitals.shape
    aux = lax.axis_size("aux")
    rows = lax.axis_size("row")
    r = lax.axis_index("row")
    width = occ_count // rows
    scale = 1.0 / (naux * aux * width) ** 0.5
    quota = 3 * own // aux
    piece = bs // 2
    chunks = own // piece
    if width % 128:
        near = [
            lax.dynamic_slice_in_dim(orbitals, jnp.clip(r + step, 0, rows - 1) * width, width, 1)
            for step in range(-2, 3)
        ]
        orbitals = jnp.stack(near, 0)
    ext = pltpu.VMEM((3 * nb, bs, width), jnp.bfloat16)
    held = pltpu.VMEM((nb, naux, bs, width), jnp.bfloat16)
    dma = pltpu.SemaphoreType.DMA
    flops = 2 * naux * bs * bs * width * nb * (3 * kept + 7 * nb)
    turned = pl.pallas_call(
        functools.partial(kernel, aux, rows, scale),
        out_shape=jax.ShapeDtypeStruct((quota, own), jnp.float32),
        in_specs=[
            pl.BlockSpec(memory_space=pltpu.SMEM),
            pl.BlockSpec(memory_space=pltpu.SMEM),
            pl.BlockSpec(memory_space=pl.ANY),
            pl.BlockSpec(memory_space=pl.ANY),
        ],
        out_specs=pl.BlockSpec(memory_space=pltpu.VMEM),
        scratch_shapes=[
            pltpu.VMEM(integrals.shape, jnp.bfloat16),
            pltpu.VMEM((5, own, width), jnp.bfloat16),
        ]
        + [ext] * 3
        + [held] * 5
        + [
            pltpu.VMEM((own, own), jnp.float32),
            pltpu.VMEM((chunks, piece, own), jnp.float32),
            pltpu.VMEM((chunks, own, piece), jnp.bfloat16),
            pltpu.VMEM((aux, quota, own), jnp.float32),
            pltpu.VMEM((aux // 2, chunks, quota, piece), jnp.bfloat16),
            dma,
            dma((5,)),
            dma((3, 2)),
            dma((3, 2)),
            dma((3, 2, aux - 1)),
            dma((3, 2, aux - 1)),
            dma((2, chunks)),
            dma((2, chunks)),
            dma((aux,)),
            dma((aux,)),
            dma((aux, chunks)),
            dma((aux, chunks)),
            dma((aux, chunks)),
            dma((aux // 2, chunks)),
        ],
        compiler_params=pltpu.CompilerParams(
            collective_id=0, has_side_effects=True, vmem_limit_bytes=48 * 1024 * 1024
        ),
        cost_estimate=pl.CostEstimate(
            flops=flops, bytes_accessed=2 * integrals.size, transcendentals=0
        ),
    )(block_columns, occ_mask, orbitals, integrals)
    return turned.T


def solution(mesh):
    in_specs = (P("aux", "row", None, None, None), P("row", None), P("row", None), P())
    out_specs = P("row", "aux")
    return jax.shard_map(
        on_device, mesh=mesh, in_specs=in_specs, out_specs=out_specs, check_vma=False
    )
```

```python
import functools

import jax
import jax.numpy as jnp
from jax import lax
from jax.experimental import pallas as pl
from jax.experimental.pallas import tpu as pltpu
from jax.sharding import PartitionSpec as P

MESH = pl.DeviceIdType.MESH
NT = (((1,), (1,)), ((), ()))


def overlap(lo, hi, start, stop):
    lo, hi = max(lo, start), min(hi, stop)
    return (lo, hi) if lo < hi else None


def kernel(
    aux,
    rows,
    scale,
    cols_hbm,
    mask_hbm,
    orb_hbm,
    int_hbm,
    out_ref,
    cols_ref,
    mask_ref,
    ints,
    orb_ref,
    e0,
    e1,
    e2,
    h0,
    h1,
    h2,
    rh0,
    rh1,
    d_buf,
    w_buf,
    v_buf,
    s_rec,
    v_rec,
    int_sem,
    small_sem,
    near_sem,
    orb_send,
    orb_recv,
    fwd_send,
    fwd_recv,
    h_send,
    h_recv,
    d_send,
    d_recv,
    w_send,
    w_recv,
    v_send,
    v_recv,
):
    a = lax.axis_index("aux")
    r = lax.axis_index("row")
    naux, nb, kept, bs, _ = ints.shape
    own = nb * bs
    width = e0.shape[-1]
    share = own // aux
    per_block = bs // share
    piece = w_buf.shape[1]
    chunks = own // piece
    half = aux // 2
    quota = out_ref.shape[0]
    low = a < half
    has_left = r > 0
    has_right = r < rows - 1
    source_row = jnp.where(low, r - 1, r + 1)
    target_row = jnp.where(low, r + 1, r - 1)
    has_source = jnp.where(low, r, rows - 1 - r) > 0
    has_target = jnp.where(low, rows - 1 - r, r) > 0
    ext = (e0, e1, e2)
    held = (h0, h1, h2)
    came = (rh0, rh1)

    load = pltpu.make_async_copy(int_hbm, ints, int_sem)
    load.start()
    small = [
        pltpu.make_async_copy(cols_hbm, cols_ref, small_sem.at[0]),
        pltpu.make_async_copy(mask_hbm, mask_ref, small_sem.at[1]),
    ]
    for copy in small:
        copy.start()
    near = []
    for t in range(5):
        if len(orb_hbm.shape) == 2:
            column = jnp.clip(r - 2 + t, 0, rows - 1) * width
            source = orb_hbm.at[:, pl.ds(pl.multiple_of(column, width), width)]
        else:
            source = orb_hbm.at[t]
        near.append(pltpu.make_async_copy(source, orb_ref.at[t], near_sem.at[t]))
        near[t].start()

    barrier = pltpu.get_barrier_semaphore()

    def greet(device):
        pl.semaphore_signal(barrier, inc=1, device_id=device, device_id_type=MESH)

    @pl.when(has_left)
    def _():
        greet((a, r - 1))

    @pl.when(has_right)
    def _():
        greet((a, r + 1))

    for step in range(1, aux):
        greet((lax.rem(a + step, aux), r))

    @pl.when(has_source)
    def _():
        for place in range(half):
            greet((jnp.where(low, half + place, place), source_row))

    greeted = jnp.where(has_left, 1, 0) + jnp.where(has_right, 1, 0)
    greeted += jnp.where(has_source, half, 0) + aux - 1
    pl.semaphore_wait(barrier, greeted)

    def remote(src, dst, send, recv, device):
        return pltpu.make_async_remote_copy(
            src_ref=src,
            dst_ref=dst,
            send_sem=send,
            recv_sem=recv,
            device_id=device,
            device_id_type=MESH,
        )

    def quarter(i, side, contributor):
        first = pl.multiple_of(lax.rem(contributor, per_block) * share, share)
        return ext[i].at[2 * nb * side + contributor // per_block, pl.ds(first, share)]

    mine = pl.ds(pl.multiple_of(a * share, share), share)

    def orb_right(i):
        return remote(
            orb_ref.at[i + 2, mine],
            quarter(i, 0, a),
            orb_send.at[i, 0],
            orb_recv.at[i, 0],
            (a, r + 1),
        )

    def orb_left(i):
        return remote(
            orb_ref.at[i, mine],
            quarter(i, 1, a),
            orb_send.at[i, 1],
            orb_recv.at[i, 1],
            (a, r - 1),
        )

    def forward(i, side, step, contributor):
        block = quarter(i, side, contributor)
        return remote(
            block,
            block,
            fwd_send.at[i, side, step - 1],
            fwd_recv.at[i, side, step - 1],
            (lax.rem(a + step, aux), r),
        )

    def send_orbitals(i):
        @pl.when(has_right)
        def _():
            orb_right(i).start()

        @pl.when(has_left)
        def _():
            orb_left(i).start()

    def share_orbitals(i):
        @pl.when(has_left)
        def _():
            orb_right(i).wait_recv()
            for step in range(1, aux):
                forward(i, 0, step, a).start()

        @pl.when(has_right)
        def _():
            orb_left(i).wait_recv()
            for step in range(1, aux):
                forward(i, 1, step, a).start()

        for b in range(nb):
            ext[i][nb + b] = orb_ref[i + 1, b * bs : (b + 1) * bs]

    def await_orbitals(i):
        for side, there in ((0, has_left), (1, has_right)):

            @pl.when(there)
            def _():
                for step in range(1, aux):
                    forward(i, side, step, lax.rem(a + aux - step, aux)).wait_recv()

    def by_half(i, act):
        if i == 0:
            act(1)
        else:

            @pl.when(low)
            def _():
                act(4 - 2 * i)

            @pl.when(jnp.logical_not(low))
            def _():
                act(2 * i - 2)

    def transform(i, b):
        by_half(i, lambda slot: transform_slot(i, slot, b))

    def transform_slot(i, slot, b):
        at = r - 1 + slot
        inside = jnp.logical_and(at >= 0, at < rows)
        held_here = mask_ref[r * nb + b, jnp.clip(at, 0, rows - 1)]
        factor = jnp.where(inside, held_here, 0).astype(jnp.float32)
        columns = [jnp.clip(cols_ref[b, k] - (r - 1) * nb, 0, 3 * nb - 1) for k in range(kept)]

        @pl.loop(0, naux)
        def _(p):
            total = jnp.zeros((bs, held[i].shape[-1]), jnp.float32)
            for k in range(kept):
                total += jnp.dot(
                    ints[p, b, k], ext[slot][columns[k]], preferred_element_type=jnp.float32
                )
            held[i][b, p] = (total * factor).astype(jnp.bfloat16)

    def piece_of(c):
        start = c * piece % bs
        return c * piece // bs, slice(start, start + piece)

    def half_copy(i, c):
        b, inner = piece_of(c)
        inner = pl.ds(inner.start, piece)
        return remote(
            held[i].at[b, :, inner],
            came[i].at[b, :, inner],
            h_send.at[i, c],
            h_recv.at[i, c],
            (a, target_row),
        )

    def send_half(i, b):
        @pl.when(has_target)
        def _():
            for c in range(b * bs // piece, (b + 1) * bs // piece):
                half_copy(i, c).start()

    def product(pairs, shape):
        def add(p, total):
            for left, lb, li, right, rb, ri in pairs:
                total += lax.dot_general(
                    left[lb, p, li], right[rb, p, ri], NT, preferred_element_type=jnp.float32
                )
            return total

        return lax.fori_loop(0, naux, add, jnp.zeros(shape, jnp.float32)) * scale

    def part_of(owner, base, start, stop):
        return overlap(base + start, base + stop, owner * quota, (owner + 1) * quota)

    def diagonal_copy(owner, contributor, span):
        lo, hi = span
        return remote(
            d_buf.at[pl.ds(lo - own, hi - lo)],
            s_rec.at[contributor, pl.ds(lo - owner * quota, hi - lo)],
            d_send.at[owner],
            d_recv.at[contributor],
            (owner, r),
        )

    def beside_copy(owner, contributor, span, base, b):
        lo, hi = span
        return remote(
            w_buf.at[b, pl.ds(lo - base - b * piece, hi - lo)],
            s_rec.at[contributor, pl.ds(lo - owner * quota, hi - lo)],
            w_send.at[owner, b],
            w_recv.at[contributor, b],
            (owner, r),
        )

    def turned_copy(owner, place, span, base, b):
        lo, hi = span
        return remote(
            v_buf.at[b, pl.ds(lo - base, hi - lo)],
            v_rec.at[place, b, pl.ds(lo - owner * quota, hi - lo)],
            v_send.at[owner, b],
            v_recv.at[place, b],
            (owner, source_row),
        )

    def each_diagonal(act):
        for owner in range(aux):
            span = part_of(owner, own, 0, own)
            if span is not None:

                @pl.when(a != owner)
                def _():
                    act(diagonal_copy(owner, a, span))

    def each_beside(b, act):
        for in_low, base in ((True, 0), (False, 2 * own)):

            @pl.when(jnp.logical_and(has_source, low if in_low else jnp.logical_not(low)))
            def _():
                for owner in range(aux):
                    span = part_of(owner, base, b * piece, (b + 1) * piece)
                    if span is not None:

                        @pl.when(a != owner)
                        def _():
                            act(beside_copy(owner, a, span, base, b))

    def each_turned(b, act):
        for in_low, base in ((True, 2 * own), (False, 0)):

            @pl.when(jnp.logical_and(has_source, low if in_low else jnp.logical_not(low)))
            def _():
                for owner in range(aux):
                    span = part_of(owner, base, 0, own)
                    if span is not None:
                        act(turned_copy(owner, lax.rem(a, half), span, base, b))

    def start(copy):
        copy.start()

    def wait_send(copy):
        copy.wait_send()

    for copy in near:
        copy.wait()
    send_orbitals(1)
    share_orbitals(1)
    for slot in (0, 2):
        send_orbitals(slot)
    load.wait()
    for copy in small:
        copy.wait()
    await_orbitals(1)
    transform(0, 0)
    send_half(0, 0)
    for slot in (0, 2):
        share_orbitals(slot)
    for b in range(1, nb):
        transform(0, b)
    by_half(1, await_orbitals)
    transform(1, 0)
    send_half(1, 0)
    for b in range(1, nb):
        send_half(0, b)
        transform(1, b)
        send_half(1, b)
    by_half(2, await_orbitals)
    for b in range(nb):
        transform(2, b)

    full = slice(0, bs)
    for b in range(nb):
        for other in range(nb):
            d_buf[b * bs : (b + 1) * bs, other * bs : (other + 1) * bs] = product(
                [(h, b, full, h, other, full) for h in held], (bs, bs)
            )
    each_diagonal(start)

    def finish_diagonal():
        for owner in range(aux):
            span = part_of(owner, own, 0, own)
            if span is not None:

                @pl.when(a == owner)
                def _():
                    lo, hi = span
                    first = owner * quota
                    total = d_buf[lo - own : hi - own]
                    for peer in range(aux):
                        if peer != owner:
                            diagonal_copy(owner, peer, span).wait_recv()
                            total += s_rec[peer, lo - first : hi - first]
                    out_ref[lo - first : hi - first] = total

    def side_of(owner):
        return (0, range(half)) if owner < half else (2 * own, range(half, aux))

    def finish_beside(c):
        for owner in range(aux):
            base, group = side_of(owner)
            span = part_of(owner, base, c * piece, (c + 1) * piece)
            if span is not None:

                @pl.when(jnp.logical_and(a == owner, has_source))
                def _():
                    lo, hi = span
                    first = owner * quota
                    shift = base + c * piece
                    total = w_buf[c, lo - shift : hi - shift]
                    for peer in group:
                        if peer != owner:
                            beside_copy(owner, peer, span, base, c).wait_recv()
                            total += s_rec[peer, lo - first : hi - first]
                    out_ref[lo - first : hi - first] += total

    def finish_turned(c):
        for owner in range(aux):
            base, _ = side_of(owner)
            span = part_of(owner, base, 0, own)
            if span is not None:

                @pl.when(jnp.logical_and(a == owner, has_source))
                def _():
                    lo, hi = span
                    first = owner * quota
                    for place in range(half):
                        turned_copy(owner, place, span, base, c).wait_recv()
                        out_ref[lo - first : hi - first, c * piece : (c + 1) * piece] += v_rec[
                            place, c, lo - first : hi - first
                        ].astype(jnp.float32)

    out_ref[...] = jnp.zeros_like(out_ref)
    for c in range(chunks):
        b, inner = piece_of(c)

        @pl.when(has_source)
        def _():
            half_copy(0, c).wait_recv()
            half_copy(1, c).wait_recv()
            for other in range(nb):
                v_buf[c, other * bs : (other + 1) * bs] = product(
                    [(h2, other, full, rh0, b, inner), (h0, other, full, rh1, b, inner)],
                    (bs, piece),
                ).astype(jnp.bfloat16)

        each_turned(c, start)

        @pl.when(has_source)
        def _():
            for other in range(nb):
                w_buf[c, :, other * bs : (other + 1) * bs] = product(
                    [(rh0, b, inner, h2, other, full), (rh1, b, inner, h0, other, full)],
                    (piece, bs),
                )

        each_beside(c, start)
        if c == 1:
            finish_diagonal()
        if c >= 1:
            finish_beside(c - 1)
            finish_turned(c - 1)

    finish_beside(chunks - 1)
    finish_turned(chunks - 1)

    for i in range(3):
        for side, there, copy in ((0, has_left, orb_left), (1, has_right, orb_right)):

            @pl.when(there)
            def _():
                copy(i).wait_send()
                for step in range(1, aux):
                    forward(i, side, step, a).wait_send()

    @pl.when(has_target)
    def _():
        for i in range(2):
            for c in range(chunks):
                half_copy(i, c).wait_send()

    each_diagonal(wait_send)
    for c in range(chunks):
        each_turned(c, wait_send)
        each_beside(c, wait_send)


def on_device(integrals, block_columns, orbitals, occ_mask):
    naux, nb, kept, bs, _ = integrals.shape
    own, occ_count = orbitals.shape
    aux = lax.axis_size("aux")
    rows = lax.axis_size("row")
    r = lax.axis_index("row")
    width = occ_count // rows
    scale = 1.0 / (naux * aux * width) ** 0.5
    quota = 3 * own // aux
    piece = bs // 2
    chunks = own // piece
    if width % 128:
        near = [
            lax.dynamic_slice_in_dim(orbitals, jnp.clip(r + step, 0, rows - 1) * width, width, 1)
            for step in range(-2, 3)
        ]
        orbitals = jnp.stack(near, 0)
    ext = pltpu.VMEM((3 * nb, bs, width), jnp.bfloat16)
    held = pltpu.VMEM((nb, naux, bs, width), jnp.bfloat16)
    dma = pltpu.SemaphoreType.DMA
    flops = 2 * naux * bs * bs * width * nb * (3 * kept + 7 * nb)
    turned = pl.pallas_call(
        functools.partial(kernel, aux, rows, scale),
        out_shape=jax.ShapeDtypeStruct((quota, own), jnp.float32),
        in_specs=[
            pl.BlockSpec(memory_space=pl.ANY),
            pl.BlockSpec(memory_space=pl.ANY),
            pl.BlockSpec(memory_space=pl.ANY),
            pl.BlockSpec(memory_space=pl.ANY),
        ],
        out_specs=pl.BlockSpec(memory_space=pltpu.VMEM),
        scratch_shapes=[
            pltpu.SMEM(block_columns.shape, jnp.int32),
            pltpu.SMEM(occ_mask.shape, jnp.int32),
            pltpu.VMEM(integrals.shape, jnp.bfloat16),
            pltpu.VMEM((5, own, width), jnp.bfloat16),
        ]
        + [ext] * 3
        + [held] * 5
        + [
            pltpu.VMEM((own, own), jnp.float32),
            pltpu.VMEM((chunks, piece, own), jnp.float32),
            pltpu.VMEM((chunks, own, piece), jnp.bfloat16),
            pltpu.VMEM((aux, quota, own), jnp.float32),
            pltpu.VMEM((aux // 2, chunks, quota, piece), jnp.bfloat16),
            dma,
            dma((2,)),
            dma((5,)),
            dma((3, 2)),
            dma((3, 2)),
            dma((3, 2, aux - 1)),
            dma((3, 2, aux - 1)),
            dma((2, chunks)),
            dma((2, chunks)),
            dma((aux,)),
            dma((aux,)),
            dma((aux, chunks)),
            dma((aux, chunks)),
            dma((aux, chunks)),
            dma((aux // 2, chunks)),
        ],
        compiler_params=pltpu.CompilerParams(
            collective_id=0, has_side_effects=True, vmem_limit_bytes=48 * 1024 * 1024
        ),
        cost_estimate=pl.CostEstimate(
            flops=flops, bytes_accessed=2 * integrals.size, transcendentals=0
        ),
    )(block_columns, occ_mask, orbitals, integrals)
    return turned.T


def solution(mesh):
    in_specs = (P("aux", "row", None, None, None), P("row", None), P("row", None), P())
    out_specs = P("row", "aux")
    return jax.shard_map(
        on_device, mesh=mesh, in_specs=in_specs, out_specs=out_specs, check_vma=False
    )
```

```python
import functools
import math

import jax
import jax.numpy as jnp
from jax import lax
from jax.experimental import pallas as pl
from jax.experimental.pallas import tpu as pltpu
from jax.sharding import PartitionSpec as P

MESH = pl.DeviceIdType.MESH
NT = (((1,), (1,)), ((), ()))


def overlap(lo, hi, start, stop):
    lo, hi = max(lo, start), min(hi, stop)
    return (lo, hi) if lo < hi else None


def kernel(
    aux,
    rows,
    scale,
    cols_hbm,
    mask_hbm,
    orb_hbm,
    int_hbm,
    out_ref,
    cols_ref,
    mask_ref,
    ints,
    orb_ref,
    e0,
    e1,
    e2,
    h0,
    h1,
    h2,
    rh0,
    rh1,
    d_buf,
    w_buf,
    v_buf,
    s_rec,
    v_rec,
    int_sem,
    small_sem,
    near_sem,
    orb_send,
    orb_recv,
    fwd_send,
    fwd_recv,
    h_send,
    h_recv,
    d_send,
    d_recv,
    w_send,
    w_recv,
    v_send,
    v_recv,
):
    a = lax.axis_index("aux")
    r = lax.axis_index("row")
    naux, nb, kept, bs, _ = ints.shape
    own = nb * bs
    width = e0.shape[-1]
    share = own // aux
    per_block = bs // share
    piece = w_buf.shape[1]
    chunks = own // piece
    half = aux // 2
    quota = out_ref.shape[0]
    low = a < half
    has_left = r > 0
    has_right = r < rows - 1
    source_row = jnp.where(low, r - 1, r + 1)
    target_row = jnp.where(low, r + 1, r - 1)
    has_source = jnp.where(low, r, rows - 1 - r) > 0
    has_target = jnp.where(low, rows - 1 - r, r) > 0
    ext = (e0, e1, e2)
    held = (h0, h1, h2)
    came = (rh0, rh1)

    load = pltpu.make_async_copy(int_hbm, ints, int_sem)
    load.start()
    small = [
        pltpu.make_async_copy(cols_hbm, cols_ref, small_sem.at[0]),
        pltpu.make_async_copy(mask_hbm, mask_ref, small_sem.at[1]),
    ]
    for copy in small:
        copy.start()
    near = []
    for t in range(5):
        if len(orb_hbm.shape) == 2:
            column = jnp.clip(r - 2 + t, 0, rows - 1) * width
            source = orb_hbm.at[:, pl.ds(pl.multiple_of(column, width), width)]
        else:
            source = orb_hbm.at[t]
        near.append(pltpu.make_async_copy(source, orb_ref.at[t], near_sem.at[t]))
        near[t].start()

    barrier = pltpu.get_barrier_semaphore()

    def greet(device):
        pl.semaphore_signal(barrier, inc=1, device_id=device, device_id_type=MESH)

    @pl.when(has_left)
    def _():
        greet((a, r - 1))

    @pl.when(has_right)
    def _():
        greet((a, r + 1))

    for step in range(1, aux):
        greet((lax.rem(a + step, aux), r))

    @pl.when(has_source)
    def _():
        for place in range(half):
            greet((jnp.where(low, half + place, place), source_row))

    greeted = jnp.where(has_left, 1, 0) + jnp.where(has_right, 1, 0)
    greeted += jnp.where(has_source, half, 0) + aux - 1
    pl.semaphore_wait(barrier, greeted)

    def remote(src, dst, send, recv, device):
        return pltpu.make_async_remote_copy(
            src_ref=src,
            dst_ref=dst,
            send_sem=send,
            recv_sem=recv,
            device_id=device,
            device_id_type=MESH,
        )

    def quarter(i, side, contributor):
        first = pl.multiple_of(lax.rem(contributor, per_block) * share, share)
        return ext[i].at[2 * nb * side + contributor // per_block, pl.ds(first, share)]

    mine = pl.ds(pl.multiple_of(a * share, share), share)

    def orb_right(i):
        return remote(
            orb_ref.at[i + 2, mine],
            quarter(i, 0, a),
            orb_send.at[i, 0],
            orb_recv.at[i, 0],
            (a, r + 1),
        )

    def orb_left(i):
        return remote(
            orb_ref.at[i, mine],
            quarter(i, 1, a),
            orb_send.at[i, 1],
            orb_recv.at[i, 1],
            (a, r - 1),
        )

    def forward(i, side, step, contributor):
        block = quarter(i, side, contributor)
        return remote(
            block,
            block,
            fwd_send.at[i, side, step - 1],
            fwd_recv.at[i, side, step - 1],
            (lax.rem(a + step, aux), r),
        )

    def send_orbitals(i):
        @pl.when(has_right)
        def _():
            orb_right(i).start()

        @pl.when(has_left)
        def _():
            orb_left(i).start()

    def share_orbitals(i):
        @pl.when(has_left)
        def _():
            orb_right(i).wait_recv()
            for step in range(1, aux):
                forward(i, 0, step, a).start()

        @pl.when(has_right)
        def _():
            orb_left(i).wait_recv()
            for step in range(1, aux):
                forward(i, 1, step, a).start()

        for b in range(nb):
            ext[i][nb + b] = orb_ref[i + 1, b * bs : (b + 1) * bs]

    def await_orbitals(i):
        for side, there in ((0, has_left), (1, has_right)):

            @pl.when(there)
            def _():
                for step in range(1, aux):
                    forward(i, side, step, lax.rem(a + aux - step, aux)).wait_recv()

    def by_half(i, act):
        if i == 0:
            act(1)
        else:

            @pl.when(low)
            def _():
                act(4 - 2 * i)

            @pl.when(jnp.logical_not(low))
            def _():
                act(2 * i - 2)

    def transform(i, b):
        by_half(i, lambda slot: transform_slot(i, slot, b))

    def transform_slot(i, slot, b):
        at = r - 1 + slot
        inside = jnp.logical_and(at >= 0, at < rows)
        held_here = mask_ref[r * nb + b, jnp.clip(at, 0, rows - 1)]
        factor = jnp.where(inside, held_here, 0).astype(jnp.float32)
        columns = [jnp.clip(cols_ref[b, k] - (r - 1) * nb, 0, 3 * nb - 1) for k in range(kept)]

        @pl.loop(0, naux)
        def _(p):
            total = jnp.zeros((bs, held[i].shape[-1]), jnp.float32)
            for k in range(kept):
                total += jnp.dot(
                    ints[p, b, k], ext[slot][columns[k]], preferred_element_type=jnp.float32
                )
            held[i][b, p] = (total * factor).astype(jnp.bfloat16)

    def piece_of(c):
        start = c * piece % bs
        return c * piece // bs, slice(start, start + piece)

    def half_copy(i, c):
        b, inner = piece_of(c)
        inner = pl.ds(inner.start, piece)
        return remote(
            held[i].at[b, :, inner],
            came[i].at[b, :, inner],
            h_send.at[i, c],
            h_recv.at[i, c],
            (a, target_row),
        )

    def send_half(i, b):
        @pl.when(has_target)
        def _():
            for c in range(b * bs // piece, (b + 1) * bs // piece):
                half_copy(i, c).start()

    def product(pairs, shape):
        def add(p, total):
            for left, lb, li, right, rb, ri in pairs:
                total += lax.dot_general(
                    left[lb, p, li], right[rb, p, ri], NT, preferred_element_type=jnp.float32
                )
            return total

        return lax.fori_loop(0, naux, add, jnp.zeros(shape, jnp.float32)) * scale

    def part_of(owner, base, start, stop):
        return overlap(base + start, base + stop, owner * quota, (owner + 1) * quota)

    def diagonal_copy(owner, contributor, span):
        lo, hi = span
        return remote(
            d_buf.at[pl.ds(lo - own, hi - lo)],
            s_rec.at[contributor, pl.ds(lo - owner * quota, hi - lo)],
            d_send.at[owner],
            d_recv.at[contributor],
            (owner, r),
        )

    def beside_copy(owner, contributor, span, base, b):
        lo, hi = span
        return remote(
            w_buf.at[b, pl.ds(lo - base - b * piece, hi - lo)],
            s_rec.at[contributor, pl.ds(lo - owner * quota, hi - lo)],
            w_send.at[owner, b],
            w_recv.at[contributor, b],
            (owner, r),
        )

    def turned_copy(owner, span, base, b):
        lo, hi = span
        return remote(
            v_buf.at[b, pl.ds(lo - base, hi - lo)],
            v_rec.at[b, pl.ds(lo - owner * quota, hi - lo)],
            v_send.at[owner, b],
            v_recv.at[b],
            (owner, source_row),
        )

    def each_diagonal(act):
        for owner in range(aux):
            span = part_of(owner, own, 0, own)
            if span is not None:

                @pl.when(a != owner)
                def _():
                    act(diagonal_copy(owner, a, span))

    def each_beside(b, act):
        for in_low, base in ((True, 0), (False, 2 * own)):

            @pl.when(jnp.logical_and(has_source, low if in_low else jnp.logical_not(low)))
            def _():
                for owner in range(aux):
                    span = part_of(owner, base, b * piece, (b + 1) * piece)
                    if span is not None:

                        @pl.when(a != owner)
                        def _():
                            act(beside_copy(owner, a, span, base, b))

    def each_turned(b, act):
        for base, other in ((0, 2 * own), (2 * own, 0)):

            @pl.when(jnp.logical_and(has_source, a == (base + b * piece) // quota))
            def _():
                for owner in range(aux):
                    span = part_of(owner, other, 0, own)
                    if span is not None:
                        act(turned_copy(owner, span, other, b))

    def start(copy):
        copy.start()

    def wait_send(copy):
        copy.wait_send()

    for copy in near:
        copy.wait()
    send_orbitals(1)
    share_orbitals(1)
    for slot in (0, 2):
        send_orbitals(slot)
    load.wait()
    for copy in small:
        copy.wait()
    await_orbitals(1)
    transform(0, 0)
    send_half(0, 0)
    for slot in (0, 2):
        share_orbitals(slot)
    for b in range(1, nb):
        transform(0, b)
    by_half(1, await_orbitals)
    transform(1, 0)
    send_half(1, 0)
    for b in range(1, nb):
        send_half(0, b)
        transform(1, b)
        send_half(1, b)
    by_half(2, await_orbitals)
    for b in range(nb):
        transform(2, b)

    full = slice(0, bs)
    for b in range(nb):
        for other in range(nb):
            d_buf[b * bs : (b + 1) * bs, other * bs : (other + 1) * bs] = product(
                [(h, b, full, h, other, full) for h in held], (bs, bs)
            )
    each_diagonal(start)

    def finish_diagonal():
        for owner in range(aux):
            span = part_of(owner, own, 0, own)
            if span is not None:

                @pl.when(a == owner)
                def _():
                    lo, hi = span
                    first = owner * quota
                    total = d_buf[lo - own : hi - own]
                    for peer in range(aux):
                        if peer != owner:
                            diagonal_copy(owner, peer, span).wait_recv()
                            total += s_rec[peer, lo - first : hi - first]
                    out_ref[lo - first : hi - first] = total

    def side_of(owner):
        return (0, range(half)) if owner < half else (2 * own, range(half, aux))

    def finish_beside(c):
        for owner in range(aux):
            base, group = side_of(owner)
            span = part_of(owner, base, c * piece, (c + 1) * piece)
            if span is not None:

                @pl.when(jnp.logical_and(a == owner, has_source))
                def _():
                    lo, hi = span
                    first = owner * quota
                    shift = base + c * piece
                    total = w_buf[c, lo - shift : hi - shift]
                    for peer in group:
                        if peer != owner:
                            beside_copy(owner, peer, span, base, c).wait_recv()
                            total += s_rec[peer, lo - first : hi - first]
                    out_ref[lo - first : hi - first] += total
                    v_buf[c] = total.T.astype(jnp.bfloat16)

    def finish_turned(c):
        for owner in range(aux):
            base, _ = side_of(owner)
            span = part_of(owner, base, 0, own)
            if span is not None:

                @pl.when(jnp.logical_and(a == owner, has_source))
                def _():
                    lo, hi = span
                    first = owner * quota
                    turned_copy(owner, span, base, c).wait_recv()
                    out_ref[lo - first : hi - first, c * piece : (c + 1) * piece] += v_rec[
                        c, lo - first : hi - first
                    ].astype(jnp.float32)

    out_ref[...] = jnp.zeros_like(out_ref)
    for c in range(chunks):
        b, inner = piece_of(c)

        @pl.when(has_source)
        def _():
            half_copy(0, c).wait_recv()
            half_copy(1, c).wait_recv()
            for other in range(nb):
                w_buf[c, :, other * bs : (other + 1) * bs] = product(
                    [(rh0, b, inner, h2, other, full), (rh1, b, inner, h0, other, full)],
                    (piece, bs),
                )

        each_beside(c, start)
        finish_beside(c)
        each_turned(c, start)
        if c == 1:
            finish_diagonal()
        if c >= 1:
            finish_turned(c - 1)

    finish_turned(chunks - 1)

    for i in range(3):
        for side, there, copy in ((0, has_left, orb_left), (1, has_right, orb_right)):

            @pl.when(there)
            def _():
                copy(i).wait_send()
                for step in range(1, aux):
                    forward(i, side, step, a).wait_send()

    @pl.when(has_target)
    def _():
        for i in range(2):
            for c in range(chunks):
                half_copy(i, c).wait_send()

    each_diagonal(wait_send)
    for c in range(chunks):
        each_turned(c, wait_send)
        each_beside(c, wait_send)


def on_device(integrals, block_columns, orbitals, occ_mask):
    naux, nb, kept, bs, _ = integrals.shape
    own, occ_count = orbitals.shape
    aux = lax.axis_size("aux")
    rows = lax.axis_size("row")
    r = lax.axis_index("row")
    width = occ_count // rows
    scale = 1.0 / (naux * aux * width) ** 0.5
    quota = 3 * own // aux
    piece = math.gcd(bs // 2, quota)
    chunks = own // piece
    if width % 128:
        near = [
            lax.dynamic_slice_in_dim(orbitals, jnp.clip(r + step, 0, rows - 1) * width, width, 1)
            for step in range(-2, 3)
        ]
        orbitals = jnp.stack(near, 0)
    ext = pltpu.VMEM((3 * nb, bs, width), jnp.bfloat16)
    held = pltpu.VMEM((nb, naux, bs, width), jnp.bfloat16)
    dma = pltpu.SemaphoreType.DMA
    flops = 2 * naux * bs * bs * width * nb * (3 * kept + 7 * nb)
    turned = pl.pallas_call(
        functools.partial(kernel, aux, rows, scale),
        out_shape=jax.ShapeDtypeStruct((quota, own), jnp.float32),
        in_specs=[
            pl.BlockSpec(memory_space=pltpu.HBM),
            pl.BlockSpec(memory_space=pltpu.HBM),
            pl.BlockSpec(memory_space=pltpu.HBM),
            pl.BlockSpec(memory_space=pltpu.HBM),
        ],
        out_specs=pl.BlockSpec(memory_space=pltpu.VMEM),
        scratch_shapes=[
            pltpu.SMEM(block_columns.shape, jnp.int32),
            pltpu.SMEM(occ_mask.shape, jnp.int32),
            pltpu.VMEM(integrals.shape, jnp.bfloat16),
            pltpu.VMEM((5, own, width), jnp.bfloat16),
        ]
        + [ext] * 3
        + [held] * 5
        + [
            pltpu.VMEM((own, own), jnp.float32),
            pltpu.VMEM((chunks, piece, own), jnp.float32),
            pltpu.VMEM((chunks, own, piece), jnp.bfloat16),
            pltpu.VMEM((aux, quota, own), jnp.float32),
            pltpu.VMEM((chunks, quota, piece), jnp.bfloat16),
            dma,
            dma((2,)),
            dma((5,)),
            dma((3, 2)),
            dma((3, 2)),
            dma((3, 2, aux - 1)),
            dma((3, 2, aux - 1)),
            dma((2, chunks)),
            dma((2, chunks)),
            dma((aux,)),
            dma((aux,)),
            dma((aux, chunks)),
            dma((aux, chunks)),
            dma((aux, chunks)),
            dma((chunks,)),
        ],
        compiler_params=pltpu.CompilerParams(
            collective_id=0, has_side_effects=True, vmem_limit_bytes=48 * 1024 * 1024
        ),
        cost_estimate=pl.CostEstimate(
            flops=flops, bytes_accessed=2 * integrals.size, transcendentals=0
        ),
    )(block_columns, occ_mask, orbitals, integrals)
    return turned.T


def solution(mesh):
    in_specs = (P("aux", "row", None, None, None), P("row", None), P("row", None), P())
    out_specs = P("row", "aux")
    return jax.shard_map(
        on_device, mesh=mesh, in_specs=in_specs, out_specs=out_specs, check_vma=False
    )
```

```python
import functools
import math

import jax
import jax.numpy as jnp
from jax import lax
from jax.experimental import pallas as pl
from jax.experimental.pallas import tpu as pltpu
from jax.sharding import PartitionSpec as P

MESH = pl.DeviceIdType.MESH
NT = (((1,), (1,)), ((), ()))


def overlap(lo, hi, start, stop):
    lo, hi = max(lo, start), min(hi, stop)
    return (lo, hi) if lo < hi else None


def kernel(
    aux,
    rows,
    scale,
    cols_hbm,
    mask_hbm,
    orb_hbm,
    int_hbm,
    out_ref,
    cols_ref,
    mask_ref,
    ints,
    orb_ref,
    e0,
    e1,
    e2,
    h0,
    h1,
    h2,
    rh0,
    rh1,
    d_buf,
    w_buf,
    v_buf,
    s_rec,
    v_rec,
    int_sem,
    small_sem,
    near_sem,
    orb_send,
    orb_recv,
    fwd_send,
    fwd_recv,
    h_send,
    h_recv,
    d_send,
    d_recv,
    w_send,
    w_recv,
    v_send,
    v_recv,
):
    a = lax.axis_index("aux")
    r = lax.axis_index("row")
    naux, nb, kept, bs, _ = ints.shape
    own = nb * bs
    width = e0.shape[-1]
    share = own // aux
    per_block = bs // share
    piece = w_buf.shape[1]
    chunks = own // piece
    half = aux // 2
    quota = out_ref.shape[0]
    low = a < half
    has_left = r > 0
    has_right = r < rows - 1
    source_row = jnp.where(low, r - 1, r + 1)
    target_row = jnp.where(low, r + 1, r - 1)
    has_source = jnp.where(low, r, rows - 1 - r) > 0
    has_target = jnp.where(low, rows - 1 - r, r) > 0
    ext = (e0, e1, e2)
    held = (h0, h1, h2)
    came = (rh0, rh1)

    load = pltpu.make_async_copy(int_hbm, ints, int_sem)
    load.start()
    small = [
        pltpu.make_async_copy(cols_hbm, cols_ref, small_sem.at[0]),
        pltpu.make_async_copy(mask_hbm, mask_ref, small_sem.at[1]),
    ]
    for copy in small:
        copy.start()
    near = []
    for t in range(5):
        if len(orb_hbm.shape) == 2:
            column = jnp.clip(r - 2 + t, 0, rows - 1) * width
            source = orb_hbm.at[:, pl.ds(pl.multiple_of(column, width), width)]
        else:
            source = orb_hbm.at[t]
        near.append(pltpu.make_async_copy(source, orb_ref.at[t], near_sem.at[t]))
        near[t].start()

    barrier = pltpu.get_barrier_semaphore()

    def greet(device):
        pl.semaphore_signal(barrier, inc=1, device_id=device, device_id_type=MESH)

    @pl.when(has_left)
    def _():
        greet((a, r - 1))

    @pl.when(has_right)
    def _():
        greet((a, r + 1))

    for step in range(1, aux):
        greet((lax.rem(a + step, aux), r))

    @pl.when(has_source)
    def _():
        for place in range(half):
            greet((jnp.where(low, half + place, place), source_row))

    greeted = jnp.where(has_left, 1, 0) + jnp.where(has_right, 1, 0)
    greeted += jnp.where(has_source, half, 0) + aux - 1
    pl.semaphore_wait(barrier, greeted)

    def remote(src, dst, send, recv, device):
        return pltpu.make_async_remote_copy(
            src_ref=src,
            dst_ref=dst,
            send_sem=send,
            recv_sem=recv,
            device_id=device,
            device_id_type=MESH,
        )

    def quarter(i, side, contributor):
        first = pl.multiple_of(lax.rem(contributor, per_block) * share, share)
        return ext[i].at[2 * nb * side + contributor // per_block, pl.ds(first, share)]

    mine = pl.ds(pl.multiple_of(a * share, share), share)

    def orb_right(i):
        return remote(
            orb_ref.at[i + 2, mine],
            quarter(i, 0, a),
            orb_send.at[i, 0],
            orb_recv.at[i, 0],
            (a, r + 1),
        )

    def orb_left(i):
        return remote(
            orb_ref.at[i, mine],
            quarter(i, 1, a),
            orb_send.at[i, 1],
            orb_recv.at[i, 1],
            (a, r - 1),
        )

    def forward(i, side, step, contributor):
        block = quarter(i, side, contributor)
        return remote(
            block,
            block,
            fwd_send.at[i, side, step - 1],
            fwd_recv.at[i, side, step - 1],
            (lax.rem(a + step, aux), r),
        )

    def send_orbitals(i):
        @pl.when(has_right)
        def _():
            orb_right(i).start()

        @pl.when(has_left)
        def _():
            orb_left(i).start()

    def share_orbitals(i):
        @pl.when(has_left)
        def _():
            orb_right(i).wait_recv()
            for step in range(1, aux):
                forward(i, 0, step, a).start()

        @pl.when(has_right)
        def _():
            orb_left(i).wait_recv()
            for step in range(1, aux):
                forward(i, 1, step, a).start()

        for b in range(nb):
            ext[i][nb + b] = orb_ref[i + 1, b * bs : (b + 1) * bs]

    def await_orbitals(i):
        for side, there in ((0, has_left), (1, has_right)):

            @pl.when(there)
            def _():
                for step in range(1, aux):
                    forward(i, side, step, lax.rem(a + aux - step, aux)).wait_recv()

    def by_half(i, act):
        if i == 0:
            act(1)
        else:

            @pl.when(low)
            def _():
                act(4 - 2 * i)

            @pl.when(jnp.logical_not(low))
            def _():
                act(2 * i - 2)

    def transform(i, b):
        by_half(i, lambda slot: transform_slot(i, slot, b))

    def transform_slot(i, slot, b):
        at = r - 1 + slot
        inside = jnp.logical_and(at >= 0, at < rows)
        held_here = mask_ref[jnp.clip(at, 0, rows - 1), r * nb + b]
        factor = jnp.where(inside, held_here, 0).astype(jnp.float32)
        columns = [jnp.clip(cols_ref[b, k] - (r - 1) * nb, 0, 3 * nb - 1) for k in range(kept)]

        @pl.loop(0, naux)
        def _(p):
            total = jnp.zeros((bs, held[i].shape[-1]), jnp.float32)
            for k in range(kept):
                total += jnp.dot(
                    ints[p, b, k], ext[slot][columns[k]], preferred_element_type=jnp.float32
                )
            held[i][b, p] = (total * factor).astype(jnp.bfloat16)

    def piece_of(c):
        start = c * piece % bs
        return c * piece // bs, slice(start, start + piece)

    def half_copy(i, c):
        b, inner = piece_of(c)
        inner = pl.ds(inner.start, piece)
        return remote(
            held[i].at[b, :, inner],
            came[i].at[b, :, inner],
            h_send.at[i, c],
            h_recv.at[i, c],
            (a, target_row),
        )

    def send_half(i, b):
        @pl.when(has_target)
        def _():
            for c in range(b * bs // piece, (b + 1) * bs // piece):
                half_copy(i, c).start()

    def product(pairs, shape):
        def add(p, total):
            for left, lb, li, right, rb, ri in pairs:
                total += lax.dot_general(
                    left[lb, p, li], right[rb, p, ri], NT, preferred_element_type=jnp.float32
                )
            return total

        return lax.fori_loop(0, naux, add, jnp.zeros(shape, jnp.float32)) * scale

    def part_of(owner, base, start, stop):
        return overlap(base + start, base + stop, owner * quota, (owner + 1) * quota)

    def diagonal_copy(owner, contributor, span):
        lo, hi = span
        return remote(
            d_buf.at[pl.ds(lo - own, hi - lo)],
            s_rec.at[contributor, pl.ds(lo - owner * quota, hi - lo)],
            d_send.at[owner],
            d_recv.at[contributor],
            (owner, r),
        )

    def beside_copy(owner, contributor, span, base, b):
        lo, hi = span
        return remote(
            w_buf.at[b, pl.ds(lo - base - b * piece, hi - lo)],
            s_rec.at[contributor, pl.ds(lo - owner * quota, hi - lo)],
            w_send.at[owner, b],
            w_recv.at[contributor, b],
            (owner, r),
        )

    def turned_copy(owner, span, base, b):
        lo, hi = span
        return remote(
            v_buf.at[b, pl.ds(lo - base, hi - lo)],
            v_rec.at[b, pl.ds(lo - owner * quota, hi - lo)],
            v_send.at[owner, b],
            v_recv.at[b],
            (owner, source_row),
        )

    def each_diagonal(act):
        for owner in range(aux):
            span = part_of(owner, own, 0, own)
            if span is not None:

                @pl.when(a != owner)
                def _():
                    act(diagonal_copy(owner, a, span))

    def each_beside(b, act):
        for in_low, base in ((True, 0), (False, 2 * own)):

            @pl.when(jnp.logical_and(has_source, low if in_low else jnp.logical_not(low)))
            def _():
                for owner in range(aux):
                    span = part_of(owner, base, b * piece, (b + 1) * piece)
                    if span is not None:

                        @pl.when(a != owner)
                        def _():
                            act(beside_copy(owner, a, span, base, b))

    def each_turned(b, act):
        for base, other in ((0, 2 * own), (2 * own, 0)):

            @pl.when(jnp.logical_and(has_source, a == (base + b * piece) // quota))
            def _():
                for owner in range(aux):
                    span = part_of(owner, other, 0, own)
                    if span is not None:
                        act(turned_copy(owner, span, other, b))

    def start(copy):
        copy.start()

    def wait_send(copy):
        copy.wait_send()

    for t in (1, 3, 2):
        near[t].wait()
    send_orbitals(1)
    for t in (0, 4):
        near[t].wait()
    share_orbitals(1)
    for slot in (0, 2):
        send_orbitals(slot)
    load.wait()
    for copy in small:
        copy.wait()
    await_orbitals(1)
    transform(0, 0)
    send_half(0, 0)
    for slot in (0, 2):
        share_orbitals(slot)
    for b in range(1, nb):
        transform(0, b)
    by_half(1, await_orbitals)
    transform(1, 0)
    send_half(1, 0)
    for b in range(1, nb):
        send_half(0, b)
        transform(1, b)
        send_half(1, b)
    by_half(2, await_orbitals)
    for b in range(nb):
        transform(2, b)

    full = slice(0, bs)
    for b in range(nb):
        for other in range(nb):
            d_buf[b * bs : (b + 1) * bs, other * bs : (other + 1) * bs] = product(
                [(h, b, full, h, other, full) for h in held], (bs, bs)
            )
    each_diagonal(start)

    def finish_diagonal():
        for owner in range(aux):
            span = part_of(owner, own, 0, own)
            if span is not None:

                @pl.when(a == owner)
                def _():
                    lo, hi = span
                    first = owner * quota
                    total = d_buf[lo - own : hi - own]
                    for peer in range(aux):
                        if peer != owner:
                            diagonal_copy(owner, peer, span).wait_recv()
                            total += s_rec[peer, lo - first : hi - first]
                    out_ref[lo - first : hi - first] = total

    def side_of(owner):
        return (0, range(half)) if owner < half else (2 * own, range(half, aux))

    def finish_beside(c):
        for owner in range(aux):
            base, group = side_of(owner)
            span = part_of(owner, base, c * piece, (c + 1) * piece)
            if span is not None:

                @pl.when(jnp.logical_and(a == owner, has_source))
                def _():
                    lo, hi = span
                    first = owner * quota
                    shift = base + c * piece
                    total = w_buf[c, lo - shift : hi - shift]
                    for peer in group:
                        if peer != owner:
                            beside_copy(owner, peer, span, base, c).wait_recv()
                            total += s_rec[peer, lo - first : hi - first]
                    out_ref[lo - first : hi - first] += total
                    v_buf[c] = total.T.astype(jnp.bfloat16)

    def finish_turned(c):
        for owner in range(aux):
            base, _ = side_of(owner)
            span = part_of(owner, base, 0, own)
            if span is not None:

                @pl.when(jnp.logical_and(a == owner, has_source))
                def _():
                    lo, hi = span
                    first = owner * quota
                    turned_copy(owner, span, base, c).wait_recv()
                    out_ref[lo - first : hi - first, c * piece : (c + 1) * piece] += v_rec[
                        c, lo - first : hi - first
                    ].astype(jnp.float32)

    out_ref[...] = jnp.zeros_like(out_ref)
    for c in range(chunks):
        b, inner = piece_of(c)

        @pl.when(has_source)
        def _():
            half_copy(0, c).wait_recv()
            half_copy(1, c).wait_recv()
            for other in range(nb):
                w_buf[c, :, other * bs : (other + 1) * bs] = product(
                    [(rh0, b, inner, h2, other, full), (rh1, b, inner, h0, other, full)],
                    (piece, bs),
                )

        each_beside(c, start)
        finish_beside(c)
        each_turned(c, start)
        if c == 1:
            finish_diagonal()
        if c >= 1:
            finish_turned(c - 1)

    finish_turned(chunks - 1)

    for i in range(3):
        for side, there, copy in ((0, has_left, orb_left), (1, has_right, orb_right)):

            @pl.when(there)
            def _():
                copy(i).wait_send()
                for step in range(1, aux):
                    forward(i, side, step, a).wait_send()

    @pl.when(has_target)
    def _():
        for i in range(2):
            for c in range(chunks):
                half_copy(i, c).wait_send()

    each_diagonal(wait_send)
    for c in range(chunks):
        each_turned(c, wait_send)
        each_beside(c, wait_send)


def on_device(integrals, block_columns, orbitals, occ_mask):
    naux, nb, kept, bs, _ = integrals.shape
    own, occ_count = orbitals.shape
    aux = lax.axis_size("aux")
    rows = lax.axis_size("row")
    r = lax.axis_index("row")
    width = occ_count // rows
    scale = 1.0 / (naux * aux * width) ** 0.5
    quota = 3 * own // aux
    piece = math.gcd(bs // 2, quota)
    chunks = own // piece
    if width % 128:
        near = [
            lax.dynamic_slice_in_dim(orbitals, jnp.clip(r + step, 0, rows - 1) * width, width, 1)
            for step in range(-2, 3)
        ]
        orbitals = jnp.stack(near, 0)
    ext = pltpu.VMEM((3 * nb, bs, width), jnp.bfloat16)
    held = pltpu.VMEM((nb, naux, bs, width), jnp.bfloat16)
    dma = pltpu.SemaphoreType.DMA
    flops = 2 * naux * bs * bs * width * nb * (3 * kept + 7 * nb)
    turned = pl.pallas_call(
        functools.partial(kernel, aux, rows, scale),
        out_shape=jax.ShapeDtypeStruct((quota, own), jnp.float32),
        in_specs=[
            pl.BlockSpec(memory_space=pltpu.HBM),
            pl.BlockSpec(memory_space=pltpu.HBM),
            pl.BlockSpec(memory_space=pltpu.HBM),
            pl.BlockSpec(memory_space=pltpu.HBM),
        ],
        out_specs=pl.BlockSpec(memory_space=pltpu.VMEM),
        scratch_shapes=[
            pltpu.SMEM(block_columns.shape, jnp.int32),
            pltpu.SMEM(occ_mask.shape[::-1], jnp.int32),
            pltpu.VMEM(integrals.shape, jnp.bfloat16),
            pltpu.VMEM((5, own, width), jnp.bfloat16),
        ]
        + [ext] * 3
        + [held] * 5
        + [
            pltpu.VMEM((own, own), jnp.float32),
            pltpu.VMEM((chunks, piece, own), jnp.float32),
            pltpu.VMEM((chunks, own, piece), jnp.bfloat16),
            pltpu.VMEM((aux, quota, own), jnp.float32),
            pltpu.VMEM((chunks, quota, piece), jnp.bfloat16),
            dma,
            dma((2,)),
            dma((5,)),
            dma((3, 2)),
            dma((3, 2)),
            dma((3, 2, aux - 1)),
            dma((3, 2, aux - 1)),
            dma((2, chunks)),
            dma((2, chunks)),
            dma((aux,)),
            dma((aux,)),
            dma((aux, chunks)),
            dma((aux, chunks)),
            dma((aux, chunks)),
            dma((chunks,)),
        ],
        compiler_params=pltpu.CompilerParams(
            collective_id=0, has_side_effects=True, vmem_limit_bytes=125 * 512 * 1024
        ),
        cost_estimate=pl.CostEstimate(
            flops=flops, bytes_accessed=2 * integrals.size, transcendentals=0
        ),
    )(block_columns, occ_mask.T, orbitals, integrals)
    return turned.T


def solution(mesh):
    in_specs = (P("aux", "row", None, None, None), P("row", None), P("row", None), P())
    out_specs = P("row", "aux")
    return jax.shard_map(
        on_device, mesh=mesh, in_specs=in_specs, out_specs=out_specs, check_vma=False
    )
```
